32 devices in a mesh: pair: 8 (over z, x), orb: 4 (over y, core).
Axes of the slice: x: 2, y: 2, z: 4, core: 2. Of those that a mesh axis runs over, the one named last changes fastest.
Arguments:
- integrals: bfloat16 [512, 8, 128, 128], P('pair'), may hold values from -6 to 6
- screen: int32 [2, 512, 8], P(None, 'pair'), may hold values from 0 to 95
- occupied: bfloat16 [12288, 32], P(('pair', 'orb')), may hold values from -0.3125 to 0.3125
- virtual: bfloat16 [12288, 512], P(('pair', 'orb')), may hold values from -1.5 to 1.5
- pair_index: int32 [2, 512], replicated, may hold values from 0 to 12287
Outputs:
- mo_block: bfloat16 [4, 256, 512, 512], P('orb', 'pair')
The draws below stay inside these ranges and needn't reach their ends.
All inputs are finite; a program needn't handle non-finite values.
Results may differ from the reference program's by a relative error of at most 0.0064.
Values may be sent and summed in bfloat16 or wider, within the bound.
A program may use at most 192 MiB of HBM per device.

```python
import jax
import jax.numpy as jnp
from jax import lax

BLK = 128
NBLK = 96
NOB = 32
NVB = 512
KB = 8
ROWS_DEV = 64
NBF = 12288
PAIRS = 512
IO = 8
N_PAIR = 8
N_ORB = 4


def set_ends(array, stream_key, smallest, high):
    place = [jax.random.randint(jax.random.fold_in(stream_key, axis), (), 0, length) for axis, length in enumerate(array.shape)]
    main_axis = array.shape.index(max(array.shape))
    neighbour = place[:main_axis] + [(place[main_axis] + 1) % array.shape[main_axis]] + place[main_axis + 1:]
    return array.at[tuple(place)].set(smallest).at[tuple(neighbour)].set(high)


def shard_levels(stream_key, extent, split, smallest, top_value):
    gain = 1.0
    for axis_at, blocks in split:
        steps = jax.random.uniform(jax.random.fold_in(jax.random.fold_in(stream_key, 6), axis_at), (blocks,), jnp.float32, smallest / len(split), top_value / len(split))
        gain = gain * jnp.repeat(jnp.exp(steps), extent[axis_at] // blocks).reshape((-1,) + (1,) * (len(extent) - 1 - axis_at))
    return gain


def bell_draw(stream_key, shape, scale, most, cuts=(), kind=jnp.bfloat16):
    drawn = scale * jax.random.normal(stream_key, shape, jnp.float32)
    if cuts:
        drawn = drawn * shard_levels(stream_key, shape, cuts, -0.22, 0.18)
    return jnp.clip(drawn, -most, most).astype(kind)


def setup_inputs(seed: int = 0) -> dict:
    streams_of = jax.random.split(jax.random.key(seed), 6)
    integrals = bell_draw(streams_of[0], (PAIRS, KB, BLK, BLK), 1.0, 6.0, ((0, 8),))
    screen = set_ends(jax.random.randint(streams_of[1], (2, PAIRS, KB), 0, NBLK), jax.random.fold_in(streams_of[1], 1), 0, NBLK - 1).astype(jnp.int32)
    occupied = bell_draw(streams_of[2], (NBF, NOB), (BLK * 3) ** -0.5, 0.3125, ((0, 32),))
    virtual = bell_draw(streams_of[3], (NBF, NVB), (ROWS_DEV * N_PAIR // 32 + 1) ** -0.5, 1.5, ((0, 32),))
    pair_index = set_ends(jax.random.randint(streams_of[4], (2, PAIRS), 0, NBF), jax.random.fold_in(streams_of[4], 1), 0, NBF - 1).astype(jnp.int32)
    return dict(integrals=integrals, screen=screen, occupied=occupied, virtual=virtual, pair_index=pair_index)


def reference(integrals, screen, occupied, virtual, pair_index):
    blocks = occupied.reshape(NBLK, BLK, NOB)

    def first_half(items):
        values, mrows, nrows = items
        coef_m = blocks[mrows].astype(jnp.float32)
        coef_n = blocks[nrows].astype(jnp.float32)
        half_one = jnp.einsum("kmn,kmi->kni", values.astype(jnp.float32), coef_m).astype(jnp.bfloat16)
        return jnp.einsum("knj,kni->ij", coef_n, half_one.astype(jnp.float32)).astype(jnp.bfloat16)

    halves = lax.map(first_half, (integrals, screen[0], screen[1]))
    left = virtual[pair_index[0]]
    right = virtual[pair_index[1]]

    def second_half(occ_index):
        column = lax.dynamic_index_in_dim(halves, occ_index, 1, keepdims=False)
        weighted = (left[:, None, :].astype(jnp.float32) * column[:, :, None].astype(jnp.float32)).astype(jnp.bfloat16)
        flat = weighted.reshape(PAIRS, NOB * NVB)
        result = jnp.dot(flat.T, right, preferred_element_type=jnp.float32)
        return result.astype(jnp.bfloat16).reshape(NOB, NVB, NVB)

    per_first = lax.map(second_half, jnp.arange(NOB, dtype=jnp.int32))
    arranged = per_first.reshape(N_ORB, IO, NOB, NVB, NVB).transpose(0, 2, 1, 3, 4)
    return arranged.reshape(N_ORB, NOB * IO, NVB, NVB)
```

```python
import functools

import jax
import jax.numpy as jnp
from jax import lax
from jax.experimental import pallas as pl
from jax.experimental.pallas import tpu as pltpu
from jax.sharding import PartitionSpec as P

BLK = 128
MESH = pl.DeviceIdType.MESH
BF = jnp.bfloat16
F32 = jnp.float32


def exchange_kernel(
    shape,
    screen_ref,
    ints_ref,
    occ_ref,
    vir_ref,
    pidx_ref,
    tab_ref,
    half_ref,
    ints,
    panel,
    by_core,
    by_x,
    from_y,
    mine_y,
    from_z,
    halves,
    outgoing,
    int_sem,
    ssem,
    rsem,
    a2a_s,
    a2a_r,
):
    n_pair, n_orb, nz, own_pairs, slots = shape
    n_dev = n_pair * n_orb
    d = lax.axis_index("pair")
    o = lax.axis_index("orb")
    z, x = d // 2, d % 2
    y, c = o // 2, o % 2
    me = d * n_orb + o
    rows = vir_ref.shape[0]
    width = vir_ref.shape[1]
    quarter = width // 4
    pairs = tab_ref.shape[2]
    count = own_pairs * slots
    i_count = occ_ref.shape[0]

    fetch = pltpu.make_async_copy(ints_ref.at[pl.ds(o * count, count)], ints, int_sem)
    fetch.start()

    per_dev = rows // BLK
    blocks = per_dev * nz

    def occ_at(xx, yy, cc):
        return ((xx * 2 + yy) * 2 + cc) * blocks

    for k in range(per_dev):
        panel[occ_at(x, y, c) + z * per_dev + k] = occ_ref[:, k * BLK : (k + 1) * BLK]

    barrier = pltpu.get_barrier_semaphore()

    def greet(k, carry):
        t = lax.rem(me + k, n_dev)
        pl.semaphore_signal(
            barrier, inc=1, device_id=(t // n_orb, t % n_orb), device_id_type=MESH
        )
        return carry

    lax.fori_loop(1, n_dev, greet, 0)
    pl.semaphore_wait(barrier, n_dev - 1)

    x_peer = (z * 2 + 1 - x, o)
    y_peer = (d, (1 - y) * 2 + c)
    c_peer = (d, y * 2 + 1 - c)
    used = [0]

    def send(src, dst, peer):
        n = used[0]
        used[0] += 1
        copy = pltpu.make_async_remote_copy(
            src_ref=src,
            dst_ref=dst,
            send_sem=ssem.at[n],
            recv_sem=rsem.at[n],
            device_id=peer,
            device_id_type=MESH,
        )
        copy.start()
        return copy

    started = []

    def z_spread(ref):
        out = []
        for k in range(1, nz):
            zz = lax.rem(z + k, nz)
            out.append(send(ref, ref, (zz * 2 + x, o)))
        return out

    occ_own = panel.at[pl.ds(occ_at(x, y, c) + z * per_dev, per_dev)]
    occ_z = z_spread(occ_own)
    half_w = 2 * quarter
    away = pl.multiple_of((1 - c) * half_w, half_w)
    home = pl.multiple_of(c * half_w, half_w)
    vir_c = send(vir_ref.at[:, pl.ds(away, half_w)], by_core.at[c], c_peer)
    by_core[c] = vir_ref[:, pl.ds(home, half_w)]
    vir_c.wait()
    away_x = pl.multiple_of((1 - x) * quarter, quarter)
    home_x = pl.multiple_of(x * quarter, quarter)
    vir_x = send(by_core.at[:, :, pl.ds(away_x, quarter)], by_x.at[x], x_peer)
    by_x[x] = by_core[:, :, pl.ds(home_x, quarter)]
    for copy in occ_z:
        copy.wait()

    def plane_first(view):
        own = view(x, y, c, None)
        return [send(own, own, peer) for peer in (x_peer, y_peer, c_peer)]

    def plane_second(view, first):
        first[0].wait()
        from_x = view(1 - x, y, c, None)
        part = view(1 - x, y, c, 0)
        out = [send(part, part, y_peer), send(from_x, from_x, c_peer)]
        first[1].wait()
        from_yy = view(x, 1 - y, c, None)
        part = view(x, 1 - y, c, 1)
        return out + [send(part, part, x_peer), send(from_yy, from_yy, c_peer)]

    def plane_third(view, first, second):
        second[0].wait()
        second[2].wait()
        diag = view(1 - x, 1 - y, c, None)
        third = send(diag, diag, c_peer)
        first[2].wait()
        second[1].wait()
        second[3].wait()
        return third

    def occ_view(xx, yy, cc, part):
        if part is None:
            return panel.at[pl.ds(occ_at(xx, yy, cc), blocks)]
        h = blocks // 2
        return panel.at[pl.ds(occ_at(xx, yy, cc) + part * h, h)]

    occ_1 = plane_first(occ_view)
    occ_2 = plane_second(occ_view, occ_1)

    vir_x.wait()

    def picked(which):
        total = jnp.zeros((pairs, quarter), F32)
        want = pidx_ref[which]
        for xx in range(2):
            for cc in range(2):
                base = ((z * 2 + xx) * n_orb + y * 2 + cc) * rows
                at = lax.broadcasted_iota(jnp.int32, (pairs, rows), 1) + base
                hot = jnp.where(at == want, 1.0, 0.0).astype(BF)
                total += jnp.dot(hot, by_x[xx, cc], preferred_element_type=F32)
        return total.astype(BF)

    mine_y[0] = picked(1 - y)
    vir_y = send(mine_y.at[0], from_y, y_peer)
    mine_y[1] = picked(y)
    vir_y.wait()
    mine_y[1] = mine_y[1] + from_y[...]
    share = pairs // nz
    vir_z = []
    for k in range(1, nz):
        zz = lax.rem(z + k, nz)
        vir_z.append(
            send(
                mine_y.at[1, pl.ds(pl.multiple_of(zz * share, share), share)],
                from_z.at[k - 1],
                (zz * 2 + x, o),
            )
        )
    occ_3 = plane_third(occ_view, occ_1, occ_2)
    for copy in vir_z:
        copy.wait()
    at_z = pl.ds(pl.multiple_of(z * share, share), share)
    total = mine_y[1, at_z]
    for k in range(nz - 1):
        total = total + from_z[k]
    tab_ref[c * 2 + x, y, at_z] = total
    tab_z = z_spread(tab_ref.at[c * 2 + x, y, at_z])

    fetch.wait()
    occ_3.wait()

    def transform(p, carry):
        firsts, seconds = [], []
        for s in range(slots):
            block_m = panel[screen_ref[0, p * slots + s]]
            first = jnp.dot(block_m, ints[p * slots + s], preferred_element_type=F32)
            firsts.append(first.astype(BF))
            seconds.append(panel[screen_ref[1, p * slots + s]])
        halves[p] = lax.dot_general(
            jnp.concatenate(seconds, axis=1),
            jnp.concatenate(firsts, axis=1),
            (((1,), (1,)), ((), ())),
            preferred_element_type=F32,
        )
        return carry

    quarter_pairs = own_pairs // 4
    lax.fori_loop(0, quarter_pairs, transform, 0)

    for copy in tab_z:
        copy.wait()

    def tab_view(xx, yy, cc, part):
        if part is None:
            return tab_ref.at[cc * 2 + xx, yy]
        h = pairs // 2
        return tab_ref.at[cc * 2 + xx, yy, pl.ds(part * h, h)]

    tab_1 = plane_first(tab_view)
    lax.fori_loop(quarter_pairs, own_pairs, transform, 0)

    flat = jnp.concatenate([halves[p] for p in range(own_pairs)], axis=1).astype(BF)
    size = own_pairs * i_count
    row = lax.broadcasted_iota(jnp.int32, (size, size), 0)
    col = lax.broadcasted_iota(jnp.int32, (size, size), 1)
    source = (col % own_pairs) * i_count + col // own_pairs
    swap = jnp.where(row == source, 1.0, 0.0).astype(BF)
    swapped = jnp.dot(flat, swap, preferred_element_type=F32)
    j_own = i_count // n_pair
    lanes = size // n_orb
    for dd in range(n_pair):
        for oo in range(n_orb):
            outgoing[dd * n_orb + oo] = swapped[
                dd * j_own : (dd + 1) * j_own, oo * lanes : (oo + 1) * lanes
            ]
    half_ref[me] = outgoing[me]

    def a2a(k):
        t = lax.rem(me + k, n_dev)
        return pltpu.make_async_remote_copy(
            src_ref=outgoing.at[t],
            dst_ref=half_ref.at[me],
            send_sem=a2a_s.at[k],
            recv_sem=a2a_r.at[k],
            device_id=(t // n_orb, t % n_orb),
            device_id_type=MESH,
        )

    def a2a_start(k, carry):
        a2a(k).start()
        return carry

    def a2a_wait(k, carry):
        a2a(k).wait()
        return carry

    lax.fori_loop(1, n_dev, a2a_start, 0)
    tab_2 = plane_second(tab_view, tab_1)
    tab_3 = plane_third(tab_view, tab_1, tab_2)
    lax.fori_loop(1, n_dev, a2a_wait, 0)
    tab_3.wait()


def expand_kernel(per_step, half_ref, tab_ref, out_ref, left_t, right):
    step = pl.program_id(0)
    width = left_t.shape[0]
    quarter = width // 4

    @pl.when(step == 0)
    def _():
        for q in range(4):
            left_t[q * quarter : (q + 1) * quarter, :] = tab_ref[q, 0].T
            right[:, q * quarter : (q + 1) * quarter] = tab_ref[q, 1]

    for k in range(per_step):
        weighted = left_t[...] * half_ref[step * per_step + k]
        out_ref[0, k] = jnp.dot(
            weighted, right[...], preferred_element_type=F32
        ).astype(BF)


def fast_body(integrals, screen, occupied, virtual, pair_index):
    n_pair, n_orb = lax.axis_size("pair"), lax.axis_size("orb")
    n_dev = n_pair * n_orb
    nz = n_pair // 2
    rows, width = virtual.shape
    pairs = pair_index.shape[1]
    i_count = occupied.shape[1]
    slots = integrals.shape[1]
    own_pairs = integrals.shape[0] // n_orb
    per_dev = rows // BLK
    own_screen = lax.dynamic_slice_in_dim(
        screen, lax.axis_index("orb") * own_pairs, own_pairs, 1
    ).reshape(2, own_pairs * slots)
    dev, k = own_screen // per_dev, own_screen % per_dev
    dz, rest = dev // (2 * n_orb), dev % (2 * n_orb)
    own_screen = (rest * nz + dz) * per_dev + k
    share = pairs // nz
    j_own = i_count // n_pair
    lanes = own_pairs * i_count // n_orb
    sends = 2 * (nz - 1) + 8 + 3 + (nz - 1) + 8
    vmem = pl.BlockSpec(memory_space=pltpu.VMEM)
    table, half = pl.pallas_call(
        functools.partial(exchange_kernel, (n_pair, n_orb, nz, own_pairs, slots)),
        out_shape=(
            jax.ShapeDtypeStruct((4, 2, pairs, width // 4), BF),
            jax.ShapeDtypeStruct((n_dev, j_own, lanes), F32),
        ),
        in_specs=[
            pl.BlockSpec(memory_space=pltpu.SMEM),
            pl.BlockSpec(memory_space=pl.ANY),
            vmem,
            vmem,
            vmem,
        ],
        out_specs=(vmem, vmem),
        scratch_shapes=[
            pltpu.VMEM((own_pairs * slots, BLK, BLK), BF),
            pltpu.VMEM((n_dev * per_dev, i_count, BLK), BF),
            pltpu.VMEM((2, rows, width // 2), BF),
            pltpu.VMEM((2, 2, rows, width // 4), BF),
            pltpu.VMEM((pairs, width // 4), BF),
            pltpu.VMEM((2, pairs, width // 4), BF),
            pltpu.VMEM((nz - 1, share, width // 4), BF),
            pltpu.VMEM((own_pairs, i_count, i_count), F32),
            pltpu.VMEM((n_dev, j_own, lanes), F32),
            pltpu.SemaphoreType.DMA,
            pltpu.SemaphoreType.DMA((sends,)),
            pltpu.SemaphoreType.DMA((sends,)),
            pltpu.SemaphoreType.DMA((n_dev,)),
            pltpu.SemaphoreType.DMA((n_dev,)),
        ],
        compiler_params=pltpu.CompilerParams(
            collective_id=0, has_side_effects=True, vmem_limit_bytes=48 * 2**20
        ),
    )(
        own_screen,
        integrals.reshape(-1, BLK, BLK),
        occupied.T,
        virtual,
        pair_index[:, :, None],
    )
    k_own = i_count // n_orb
    half = half.reshape(n_dev, j_own, k_own, own_pairs).transpose(1, 2, 0, 3)
    half = half.reshape(j_own * k_own, 1, pairs).astype(BF)
    count = j_own * k_own
    per_step = 2
    return pl.pallas_call(
        functools.partial(expand_kernel, per_step),
        grid=(count // per_step,),
        out_shape=jax.ShapeDtypeStruct((1, count, width, width), BF),
        in_specs=[vmem, vmem],
        out_specs=pl.BlockSpec((1, per_step, width, width), lambda s: (0, s, 0, 0)),
        scratch_shapes=[pltpu.VMEM((width, pairs), BF), pltpu.VMEM((pairs, width), BF)],
        compiler_params=pltpu.CompilerParams(vmem_limit_bytes=48 * 2**20),
    )(half, table)


def plain_body(integrals, screen, occupied, virtual, pair_index):
    occ_all = lax.all_gather(occupied, ("pair", "orb"), axis=0, tiled=True)
    vir_all = lax.all_gather(virtual, ("pair", "orb"), axis=0, tiled=True)
    first_count = occ_all.shape[1] // lax.axis_size("orb")
    own_cols = lax.dynamic_slice_in_dim(
        occ_all, lax.axis_index("orb") * first_count, first_count, 1
    )
    block_count = occ_all.shape[0] // BLK

    def blocks_of(cols, index):
        hot = jax.nn.one_hot(index.reshape(-1), block_count, dtype=BF)
        taken = jnp.dot(
            hot, cols.reshape(block_count, -1), preferred_element_type=F32
        ).astype(BF)
        return taken.reshape(index.shape + (BLK, cols.shape[1]))

    coef_m = blocks_of(own_cols, screen[0])
    coef_n = blocks_of(occ_all, screen[1])
    half_one = jnp.einsum(
        "pkmn,pkmi->pkni", integrals, coef_m, preferred_element_type=F32
    ).astype(BF)
    half = jnp.einsum(
        "pknj,pkni->pji", coef_n, half_one, preferred_element_type=F32
    ).astype(BF)
    local_rows = half.reshape(half.shape[0], -1)
    owned = lax.all_to_all(local_rows, "pair", split_axis=1, concat_axis=0, tiled=True)
    left = vir_all[pair_index[0]]
    right = vir_all[pair_index[1]]
    weighted = (left[:, None, :].astype(F32) * owned[:, :, None].astype(F32)).astype(BF)
    width = weighted.shape[2]
    flat = weighted.reshape(weighted.shape[0], -1)
    result = lax.dot_general(
        flat, right, (((0,), (0,)), ((), ())), preferred_element_type=F32
    )
    return result.astype(BF).reshape(1, -1, width, width)


def body(*args):
    n_pair, n_orb = lax.axis_size("pair"), lax.axis_size("orb")
    fits = (
        n_orb == 4
        and n_pair % 2 == 0
        and n_pair <= 8
        and args[2].shape[0] % BLK == 0
        and args[4].shape[1] == n_pair * args[0].shape[0]
    )
    return fast_body(*args) if fits else plain_body(*args)


def solution(mesh):
    placed = (
        P("pair", None, None, None),
        P(None, "pair", None),
        P(("pair", "orb"), None),
        P(("pair", "orb"), None),
        P(),
    )
    return jax.shard_map(
        body, mesh=mesh, in_specs=placed, out_specs=P("orb", "pair", None, None), check_vma=False
    )
```

```python
import functools

import jax
import jax.numpy as jnp
from jax import lax
from jax.experimental import pallas as pl
from jax.experimental.pallas import tpu as pltpu
from jax.sharding import PartitionSpec as P

BLK = 128
MESH = pl.DeviceIdType.MESH
BF = jnp.bfloat16
F32 = jnp.float32


def exchange_kernel(
    shape,
    screen_ref,
    ints_ref,
    occ_ref,
    vir_ref,
    pidx_ref,
    tab_ref,
    half_ref,
    ints,
    panel,
    got,
    from_c,
    mine,
    from_z,
    halves,
    outgoing,
    int_sem,
    own_sem,
    ssem,
    rsem,
    a2a_s,
    a2a_r,
):
    n_pair, n_orb, nz, own_pairs, slots = shape
    n_dev = n_pair * n_orb
    d = lax.axis_index("pair")
    o = lax.axis_index("orb")
    z, x = d // 2, d % 2
    y, c = o // 2, o % 2
    me = d * n_orb + o
    rows = vir_ref.shape[0]
    pairs = tab_ref.shape[2]
    count = own_pairs * slots
    i_count = occ_ref.shape[0]

    fetch = pltpu.make_async_copy(ints_ref.at[pl.ds(o * count, count)], ints, int_sem)
    fetch.start()
    quarter = vir_ref.shape[1] // 4

    def columns(xx, yy):
        return pl.ds(pl.multiple_of((xx * 2 + yy) * quarter, quarter), quarter)

    vir_own = pltpu.make_async_copy(
        vir_ref.at[:, columns(x, y)], got.at[x * 2 + y], own_sem.at[0]
    )
    vir_own.start()

    per_dev = rows // BLK
    blocks = per_dev * nz

    def occ_at(xx, yy, cc):
        return ((xx * 2 + yy) * 2 + cc) * blocks

    occ_own = [
        pltpu.make_async_copy(
            occ_ref.at[:, k * BLK : (k + 1) * BLK],
            panel.at[occ_at(x, y, c) + z * per_dev + k],
            own_sem.at[1 + k],
        )
        for k in range(per_dev)
    ]
    for copy in occ_own:
        copy.start()

    barrier = pltpu.get_barrier_semaphore()

    def greet(k, carry):
        t = lax.rem(me + k, n_dev)
        pl.semaphore_signal(
            barrier, inc=1, device_id=(t // n_orb, t % n_orb), device_id_type=MESH
        )
        return carry

    lax.fori_loop(1, n_dev, greet, 0)
    pl.semaphore_wait(barrier, n_dev - 1)

    x_peer = (z * 2 + 1 - x, o)
    y_peer = (d, (1 - y) * 2 + c)
    c_peer = (d, y * 2 + 1 - c)
    far_peer = (z * 2 + 1 - x, (1 - y) * 2 + c)
    used = [0]

    def send(src, dst, peer):
        n = used[0]
        used[0] += 1
        copy = pltpu.make_async_remote_copy(
            src_ref=src,
            dst_ref=dst,
            send_sem=ssem.at[n],
            recv_sem=rsem.at[n],
            device_id=peer,
            device_id_type=MESH,
        )
        copy.start()
        return copy


    def z_spread(ref):
        out = []
        for k in range(1, nz):
            zz = lax.rem(z + k, nz)
            out.append(send(ref, ref, (zz * 2 + x, o)))
        return out

    vir_plane = [
        send(vir_ref.at[:, columns(xx, yy)], got.at[x * 2 + y], peer)
        for xx, yy, peer in (
            (1 - x, y, x_peer),
            (x, 1 - y, y_peer),
            (1 - x, 1 - y, far_peer),
        )
    ]
    for copy in occ_own:
        copy.wait()
    occ_own = panel.at[pl.ds(occ_at(x, y, c) + z * per_dev, per_dev)]
    occ_z = z_spread(occ_own)
    for copy in occ_z:
        copy.wait()

    def plane_first(view):
        own = view(x, y, c, None)
        return [send(own, own, peer) for peer in (x_peer, y_peer, c_peer)]

    def plane_second(view, first):
        first[0].wait()
        from_x = view(1 - x, y, c, None)
        part = view(1 - x, y, c, 0)
        out = [send(part, part, y_peer), send(from_x, from_x, c_peer)]
        first[1].wait()
        from_yy = view(x, 1 - y, c, None)
        part = view(x, 1 - y, c, 1)
        return out + [send(part, part, x_peer), send(from_yy, from_yy, c_peer)]

    def plane_third(view, first, second):
        second[0].wait()
        second[2].wait()
        diag = view(1 - x, 1 - y, c, None)
        third = send(diag, diag, c_peer)
        first[2].wait()
        second[1].wait()
        second[3].wait()
        return third

    def occ_view(xx, yy, cc, part):
        if part is None:
            return panel.at[pl.ds(occ_at(xx, yy, cc), blocks)]
        h = blocks // 2
        return panel.at[pl.ds(occ_at(xx, yy, cc) + part * h, h)]

    occ_1 = plane_first(occ_view)
    vir_own.wait()
    for copy in vir_plane:
        copy.wait()

    def picked(which):
        total = jnp.zeros((pairs, quarter), F32)
        want = jnp.broadcast_to(pidx_ref[pl.ds(which, 1)], (8, pairs)).T[:, :1]
        for xx in range(2):
            for yy in range(2):
                base = ((z * 2 + xx) * n_orb + yy * 2 + c) * rows
                at = lax.broadcasted_iota(jnp.int32, (pairs, rows), 1) + base
                hot = jnp.where(at == want, 1.0, 0.0).astype(BF)
                total += jnp.dot(hot, got[xx * 2 + yy], preferred_element_type=F32)
        return total.astype(BF)

    mine[0] = picked(1 - c)
    vir_c = send(mine.at[0], from_c, c_peer)
    mine[1] = picked(c)
    occ_2 = plane_second(occ_view, occ_1)
    vir_c.wait()
    mine[1] = mine[1] + from_c[...]
    share = pairs // nz
    vir_z = []
    for k in range(1, nz):
        zz = lax.rem(z + k, nz)
        vir_z.append(
            send(
                mine.at[1, pl.ds(pl.multiple_of(zz * share, share), share)],
                from_z.at[k - 1],
                (zz * 2 + x, o),
            )
        )
    occ_3 = plane_third(occ_view, occ_1, occ_2)
    for copy in vir_z:
        copy.wait()
    def rows_of(k):
        zz = lax.rem(z - k + nz, nz)
        return pl.ds(pl.multiple_of(zz * share, share), share)

    def tab_at(xx, yy, cc, k=None):
        if k is None:
            return tab_ref.at[xx * 2 + yy, cc]
        return tab_ref.at[xx * 2 + yy, cc, rows_of(k)]

    total = mine[1, rows_of(0)]
    for k in range(nz - 1):
        total = total + from_z[k]
    tab_ref[x * 2 + y, c, rows_of(0)] = total
    tab_z = z_spread(tab_at(x, y, c, 0))
    tab_plane = []

    def pass_on(k):
        part = tab_at(x, y, c, k)
        tab_plane.append([send(part, part, p) for p in (x_peer, y_peer, c_peer)])

    pass_on(0)

    fetch.wait()
    occ_3.wait()

    def place(block):
        dev, k = lax.div(block, per_dev), lax.rem(block, per_dev)
        dz, rest = lax.div(dev, 2 * n_orb), lax.rem(dev, 2 * n_orb)
        return rest * blocks + dz * per_dev + k

    def transform(p, carry):
        firsts, seconds = [], []
        for s in range(slots):
            block_m = panel[place(screen_ref[0, s, o * own_pairs + p])]
            first = jnp.dot(block_m, ints[p * slots + s], preferred_element_type=F32)
            firsts.append(first.astype(BF))
            seconds.append(panel[place(screen_ref[1, s, o * own_pairs + p])])
        halves[p] = lax.dot_general(
            jnp.concatenate(seconds, axis=1),
            jnp.concatenate(firsts, axis=1),
            (((1,), (1,)), ((), ())),
            preferred_element_type=F32,
        )
        return carry

    cut = own_pairs // 4
    lax.fori_loop(0, cut, transform, 0, unroll=2)
    for k in range(1, nz):
        tab_z[k - 1].wait()
        pass_on(k)
    lax.fori_loop(cut, 2 * cut, transform, 0, unroll=2)
    second = []
    for k in range(nz // 2):
        tab_plane[k][0].wait()
        part = tab_at(1 - x, y, c, k)
        second.append(send(part, part, y_peer))
        tab_plane[k][1].wait()
    lax.fori_loop(2 * cut, 3 * cut, transform, 0, unroll=2)
    for k in range(nz // 2, nz):
        tab_plane[k][1].wait()
        part = tab_at(x, 1 - y, c, k)
        second.append(send(part, part, x_peer))
        tab_plane[k][0].wait()
    across = [
        send(tab_at(1 - x, y, c), tab_at(1 - x, y, c), c_peer),
        send(tab_at(x, 1 - y, c), tab_at(x, 1 - y, c), c_peer),
    ]
    lax.fori_loop(3 * cut, own_pairs, transform, 0, unroll=2)

    flat = jnp.concatenate([halves[p] for p in range(own_pairs)], axis=1).astype(BF)
    size = own_pairs * i_count
    row = lax.broadcasted_iota(jnp.int32, (size, size), 0)
    col = lax.broadcasted_iota(jnp.int32, (size, size), 1)
    source = (col % own_pairs) * i_count + col // own_pairs
    swap = jnp.where(row == source, 1.0, 0.0).astype(BF)
    swapped = jnp.dot(flat, swap, preferred_element_type=F32)
    j_own = i_count // n_pair
    lanes = size // n_orb
    for dd in range(n_pair):
        for oo in range(n_orb):
            outgoing[dd * n_orb + oo] = swapped[
                dd * j_own : (dd + 1) * j_own, oo * lanes : (oo + 1) * lanes
            ]
    half_ref[me] = outgoing[me]

    def a2a(k):
        t = lax.rem(me + k, n_dev)
        return pltpu.make_async_remote_copy(
            src_ref=outgoing.at[t],
            dst_ref=half_ref.at[me],
            send_sem=a2a_s.at[k],
            recv_sem=a2a_r.at[k],
            device_id=(t // n_orb, t % n_orb),
            device_id_type=MESH,
        )

    def a2a_start(k, carry):
        a2a(k).start()
        return carry

    def a2a_wait(k, carry):
        a2a(k).wait()
        return carry

    lax.fori_loop(1, n_dev, a2a_start, 0)
    for copy in second:
        copy.wait()
    far = tab_at(1 - x, 1 - y, c)
    across.append(send(far, far, c_peer))
    for group in tab_plane:
        group[2].wait()
    lax.fori_loop(1, n_dev, a2a_wait, 0)
    for copy in across:
        copy.wait()


def expand_kernel(per_step, half_ref, tab_ref, out_ref, left_t, right):
    step = pl.program_id(0)
    width = left_t.shape[0]
    quarter = width // 4

    @pl.when(step == 0)
    def _():
        for q in range(4):
            left_t[q * quarter : (q + 1) * quarter, :] = tab_ref[q, 0].T
            right[:, q * quarter : (q + 1) * quarter] = tab_ref[q, 1]

    for k in range(per_step):
        weighted = left_t[...] * half_ref[step * per_step + k]
        out_ref[0, k] = jnp.dot(
            weighted, right[...], preferred_element_type=F32
        ).astype(BF)


def fast_body(integrals, screen, occupied, virtual, pair_index):
    n_pair, n_orb = lax.axis_size("pair"), lax.axis_size("orb")
    n_dev = n_pair * n_orb
    nz = n_pair // 2
    rows, width = virtual.shape
    pairs = pair_index.shape[1]
    i_count = occupied.shape[1]
    slots = integrals.shape[1]
    own_pairs = integrals.shape[0] // n_orb
    per_dev = rows // BLK
    share = pairs // nz
    j_own = i_count // n_pair
    lanes = own_pairs * i_count // n_orb
    sends = 3 + 3 * (nz - 1) + 8 + 1 + 4 * nz + 3
    vmem = pl.BlockSpec(memory_space=pltpu.VMEM)
    table, half = pl.pallas_call(
        functools.partial(exchange_kernel, (n_pair, n_orb, nz, own_pairs, slots)),
        out_shape=(
            jax.ShapeDtypeStruct((4, 2, pairs, width // 4), BF),
            jax.ShapeDtypeStruct((n_dev, j_own, lanes), F32),
        ),
        in_specs=[
            pl.BlockSpec(memory_space=pltpu.SMEM),
            pl.BlockSpec(memory_space=pltpu.HBM),
            pl.BlockSpec(memory_space=pltpu.HBM),
            pl.BlockSpec(memory_space=pltpu.HBM),
            vmem,
        ],
        out_specs=(vmem, vmem),
        scratch_shapes=[
            pltpu.VMEM((own_pairs * slots, BLK, BLK), BF),
            pltpu.VMEM((n_dev * per_dev, i_count, BLK), BF),
            pltpu.VMEM((4, rows, width // 4), BF),
            pltpu.VMEM((pairs, width // 4), BF),
            pltpu.VMEM((2, pairs, width // 4), BF),
            pltpu.VMEM((nz - 1, share, width // 4), BF),
            pltpu.VMEM((own_pairs, i_count, i_count), F32),
            pltpu.VMEM((n_dev, j_own, lanes), F32),
            pltpu.SemaphoreType.DMA,
            pltpu.SemaphoreType.DMA((1 + per_dev,)),
            pltpu.SemaphoreType.DMA((sends,)),
            pltpu.SemaphoreType.DMA((sends,)),
            pltpu.SemaphoreType.DMA((n_dev,)),
            pltpu.SemaphoreType.DMA((n_dev,)),
        ],
        compiler_params=pltpu.CompilerParams(
            collective_id=0, has_side_effects=True, vmem_limit_bytes=60 * 2**20
        ),
    )(
        screen.transpose(0, 2, 1),
        integrals.reshape(-1, BLK, BLK),
        occupied.T,
        virtual,
        pair_index,
    )
    k_own = i_count // n_orb
    half = half.reshape(n_dev, j_own, k_own, own_pairs).transpose(1, 2, 0, 3)
    half = half.reshape(j_own * k_own, 1, pairs).astype(BF)
    count = j_own * k_own
    per_step = 8
    return pl.pallas_call(
        functools.partial(expand_kernel, per_step),
        grid=(count // per_step,),
        out_shape=jax.ShapeDtypeStruct((1, count, width, width), BF),
        in_specs=[vmem, vmem],
        out_specs=pl.BlockSpec((1, per_step, width, width), lambda s: (0, s, 0, 0)),
        scratch_shapes=[pltpu.VMEM((width, pairs), BF), pltpu.VMEM((pairs, width), BF)],
        compiler_params=pltpu.CompilerParams(vmem_limit_bytes=60 * 2**20),
    )(half, table)


def plain_body(integrals, screen, occupied, virtual, pair_index):
    occ_all = lax.all_gather(occupied, ("pair", "orb"), axis=0, tiled=True)
    vir_all = lax.all_gather(virtual, ("pair", "orb"), axis=0, tiled=True)
    first_count = occ_all.shape[1] // lax.axis_size("orb")
    own_cols = lax.dynamic_slice_in_dim(
        occ_all, lax.axis_index("orb") * first_count, first_count, 1
    )
    block_count = occ_all.shape[0] // BLK

    def blocks_of(cols, index):
        hot = jax.nn.one_hot(index.reshape(-1), block_count, dtype=BF)
        taken = jnp.dot(
            hot, cols.reshape(block_count, -1), preferred_element_type=F32
        ).astype(BF)
        return taken.reshape(index.shape + (BLK, cols.shape[1]))

    coef_m = blocks_of(own_cols, screen[0])
    coef_n = blocks_of(occ_all, screen[1])
    half_one = jnp.einsum(
        "pkmn,pkmi->pkni", integrals, coef_m, preferred_element_type=F32
    ).astype(BF)
    half = jnp.einsum(
        "pknj,pkni->pji", coef_n, half_one, preferred_element_type=F32
    ).astype(BF)
    local_rows = half.reshape(half.shape[0], -1)
    owned = lax.all_to_all(local_rows, "pair", split_axis=1, concat_axis=0, tiled=True)
    left = vir_all[pair_index[0]]
    right = vir_all[pair_index[1]]
    weighted = (left[:, None, :].astype(F32) * owned[:, :, None].astype(F32)).astype(BF)
    width = weighted.shape[2]
    flat = weighted.reshape(weighted.shape[0], -1)
    result = lax.dot_general(
        flat, right, (((0,), (0,)), ((), ())), preferred_element_type=F32
    )
    return result.astype(BF).reshape(1, -1, width, width)


def body(*args):
    n_pair, n_orb = lax.axis_size("pair"), lax.axis_size("orb")
    fits = (
        n_orb == 4
        and n_pair in (4, 8)
        and args[2].shape[0] % BLK == 0
        and args[4].shape[1] == n_pair * args[0].shape[0]
    )
    return fast_body(*args) if fits else plain_body(*args)


def solution(mesh):
    placed = (
        P("pair", None, None, None),
        P(None, "pair", None),
        P(("pair", "orb"), None),
        P(("pair", "orb"), None),
        P(),
    )
    return jax.shard_map(
        body, mesh=mesh, in_specs=placed, out_specs=P("orb", "pair", None, None), check_vma=False
    )
```

```python
import functools

import jax
import jax.numpy as jnp
from jax import lax
from jax.experimental import pallas as pl
from jax.experimental.pallas import tpu as pltpu
from jax.sharding import PartitionSpec as P

BLK = 128
MESH = pl.DeviceIdType.MESH
BF = jnp.bfloat16
F32 = jnp.float32


def exchange_kernel(
    shape,
    screen_ref,
    ints_ref,
    occ_ref,
    vir_ref,
    pidx_ref,
    tab_ref,
    half_ref,
    ints,
    panel,
    got,
    from_c,
    mine,
    from_z,
    halves,
    outgoing,
    int_sem,
    own_sem,
    ssem,
    rsem,
    a2a_s,
    a2a_r,
):
    n_pair, n_orb, nz, own_pairs, slots = shape
    n_dev = n_pair * n_orb
    d = lax.axis_index("pair")
    o = lax.axis_index("orb")
    z, x = d // 2, d % 2
    y, c = o // 2, o % 2
    me = d * n_orb + o
    rows = vir_ref.shape[0]
    pairs = tab_ref.shape[2]
    count = own_pairs * slots
    i_count = occ_ref.shape[0]

    fetch = pltpu.make_async_copy(ints_ref.at[pl.ds(o * count, count)], ints, int_sem)
    fetch.start()
    quarter = vir_ref.shape[1] // 4

    def columns(xx, yy):
        return pl.ds(pl.multiple_of((xx * 2 + yy) * quarter, quarter), quarter)

    vir_own = pltpu.make_async_copy(
        vir_ref.at[:, columns(x, y)], got.at[x * 2 + y], own_sem.at[0]
    )
    vir_own.start()

    per_dev = rows // BLK
    blocks = per_dev * nz

    def occ_at(xx, yy, cc):
        return ((xx * 2 + yy) * 2 + cc) * blocks

    occ_own = [
        pltpu.make_async_copy(
            occ_ref.at[:, k * BLK : (k + 1) * BLK],
            panel.at[occ_at(x, y, c) + z * per_dev + k],
            own_sem.at[1 + k],
        )
        for k in range(per_dev)
    ]
    for copy in occ_own:
        copy.start()

    barrier = pltpu.get_barrier_semaphore()

    def greet(k, carry):
        t = lax.rem(me + k, n_dev)
        pl.semaphore_signal(
            barrier, inc=1, device_id=(t // n_orb, t % n_orb), device_id_type=MESH
        )
        return carry

    lax.fori_loop(1, n_dev, greet, 0)
    pl.semaphore_wait(barrier, n_dev - 1)

    x_peer = (z * 2 + 1 - x, o)
    y_peer = (d, (1 - y) * 2 + c)
    c_peer = (d, y * 2 + 1 - c)
    far_peer = (z * 2 + 1 - x, (1 - y) * 2 + c)
    used = [0]

    def send(src, dst, peer):
        n = used[0]
        used[0] += 1
        copy = pltpu.make_async_remote_copy(
            src_ref=src,
            dst_ref=dst,
            send_sem=ssem.at[n],
            recv_sem=rsem.at[n],
            device_id=peer,
            device_id_type=MESH,
        )
        copy.start()
        return copy


    def z_spread(ref):
        out = []
        for k in range(1, nz):
            zz = lax.rem(z + k, nz)
            out.append(send(ref, ref, (zz * 2 + x, o)))
        return out

    vir_plane = [
        send(vir_ref.at[:, columns(xx, yy)], got.at[x * 2 + y], peer)
        for xx, yy, peer in (
            (1 - x, y, x_peer),
            (x, 1 - y, y_peer),
            (1 - x, 1 - y, far_peer),
        )
    ]
    for copy in occ_own:
        copy.wait()
    occ_own = panel.at[pl.ds(occ_at(x, y, c) + z * per_dev, per_dev)]
    occ_z = z_spread(occ_own)
    for copy in occ_z:
        copy.wait()

    def plane_first(view):
        own = view(x, y, c, None)
        return [send(own, own, peer) for peer in (x_peer, y_peer, c_peer)]

    def plane_second(view, first):
        first[0].wait()
        from_x = view(1 - x, y, c, None)
        part = view(1 - x, y, c, 0)
        out = [send(part, part, y_peer), send(from_x, from_x, c_peer)]
        first[1].wait()
        from_yy = view(x, 1 - y, c, None)
        part = view(x, 1 - y, c, 1)
        return out + [send(part, part, x_peer), send(from_yy, from_yy, c_peer)]

    def plane_third(view, first, second):
        second[0].wait()
        second[2].wait()
        diag = view(1 - x, 1 - y, c, None)
        third = send(diag, diag, c_peer)
        first[2].wait()
        second[1].wait()
        second[3].wait()
        return third

    def occ_view(xx, yy, cc, part):
        if part is None:
            return panel.at[pl.ds(occ_at(xx, yy, cc), blocks)]
        h = blocks // 2
        return panel.at[pl.ds(occ_at(xx, yy, cc) + part * h, h)]

    occ_1 = plane_first(occ_view)
    vir_own.wait()
    for copy in vir_plane:
        copy.wait()

    def picked(which):
        total = jnp.zeros((pairs, quarter), F32)
        want = jnp.broadcast_to(pidx_ref[pl.ds(which, 1)], (8, pairs)).T[:, :1]
        for xx in range(2):
            for yy in range(2):
                base = ((z * 2 + xx) * n_orb + yy * 2 + c) * rows
                at = lax.broadcasted_iota(jnp.int32, (pairs, rows), 1) + base
                hot = jnp.where(at == want, 1.0, 0.0).astype(BF)
                total += jnp.dot(hot, got[xx * 2 + yy], preferred_element_type=F32)
        return total.astype(BF)

    mine[0] = picked(1 - c)
    vir_c = send(mine.at[0], from_c, c_peer)
    mine[1] = picked(c)
    occ_2 = plane_second(occ_view, occ_1)
    vir_c.wait()
    mine[1] = mine[1] + from_c[...]
    share = pairs // nz
    vir_z = []
    for k in range(1, nz):
        zz = lax.rem(z + k, nz)
        vir_z.append(
            send(
                mine.at[1, pl.ds(pl.multiple_of(zz * share, share), share)],
                from_z.at[k - 1],
                (zz * 2 + x, o),
            )
        )
    occ_3 = plane_third(occ_view, occ_1, occ_2)
    fetch.wait()
    occ_3.wait()

    def place(block):
        dev, k = lax.div(block, per_dev), lax.rem(block, per_dev)
        dz, rest = lax.div(dev, 2 * n_orb), lax.rem(dev, 2 * n_orb)
        return rest * blocks + dz * per_dev + k

    def transform(p, carry):
        firsts, seconds = [], []
        for s in range(slots):
            block_m = panel[place(screen_ref[0, s, o * own_pairs + p])]
            first = jnp.dot(block_m, ints[p * slots + s], preferred_element_type=F32)
            firsts.append(first.astype(BF))
            seconds.append(panel[place(screen_ref[1, s, o * own_pairs + p])])
        halves[p] = lax.dot_general(
            jnp.concatenate(seconds, axis=1),
            jnp.concatenate(firsts, axis=1),
            (((1,), (1,)), ((), ())),
            preferred_element_type=F32,
        )
        return carry

    cut = own_pairs // 4
    lax.fori_loop(0, cut, transform, 0, unroll=2)
    for copy in vir_z:
        copy.wait()
    def rows_of(k):
        zz = lax.rem(z - k + nz, nz)
        return pl.ds(pl.multiple_of(zz * share, share), share)

    def tab_at(xx, yy, cc, k=None):
        if k is None:
            return tab_ref.at[xx * 2 + yy, cc]
        return tab_ref.at[xx * 2 + yy, cc, rows_of(k)]

    total = mine[1, rows_of(0)]
    for k in range(nz - 1):
        total = total + from_z[k]
    tab_ref[x * 2 + y, c, rows_of(0)] = total
    tab_z = z_spread(tab_at(x, y, c, 0))
    tab_plane = []

    def pass_on(k):
        part = tab_at(x, y, c, k)
        tab_plane.append([send(part, part, p) for p in (x_peer, y_peer, c_peer)])

    pass_on(0)

    lax.fori_loop(cut, 3 * cut, transform, 0, unroll=2)
    for k in range(1, nz):
        tab_z[k - 1].wait()
        pass_on(k)
    lax.fori_loop(3 * cut, own_pairs, transform, 0, unroll=2)
    second = []
    for k in range(nz // 2):
        tab_plane[k][0].wait()
        part = tab_at(1 - x, y, c, k)
        second.append(send(part, part, y_peer))
        tab_plane[k][1].wait()
    for k in range(nz // 2, nz):
        tab_plane[k][1].wait()
        part = tab_at(x, 1 - y, c, k)
        second.append(send(part, part, x_peer))
        tab_plane[k][0].wait()
    across = [
        send(tab_at(1 - x, y, c), tab_at(1 - x, y, c), c_peer),
        send(tab_at(x, 1 - y, c), tab_at(x, 1 - y, c), c_peer),
    ]

    flat = jnp.concatenate([halves[p] for p in range(own_pairs)], axis=1).astype(BF)
    size = own_pairs * i_count
    row = lax.broadcasted_iota(jnp.int32, (size, size), 0)
    col = lax.broadcasted_iota(jnp.int32, (size, size), 1)
    source = (col % own_pairs) * i_count + col // own_pairs
    swap = jnp.where(row == source, 1.0, 0.0).astype(BF)
    swapped = jnp.dot(flat, swap, preferred_element_type=F32)
    j_own = i_count // n_pair
    lanes = size // n_orb
    for dd in range(n_pair):
        for oo in range(n_orb):
            outgoing[dd * n_orb + oo] = swapped[
                dd * j_own : (dd + 1) * j_own, oo * lanes : (oo + 1) * lanes
            ]
    half_ref[me] = outgoing[me]

    def a2a(k):
        t = lax.rem(me + k, n_dev)
        return pltpu.make_async_remote_copy(
            src_ref=outgoing.at[t],
            dst_ref=half_ref.at[me],
            send_sem=a2a_s.at[k],
            recv_sem=a2a_r.at[k],
            device_id=(t // n_orb, t % n_orb),
            device_id_type=MESH,
        )

    def a2a_start(k, carry):
        a2a(k).start()
        return carry

    def a2a_wait(k, carry):
        a2a(k).wait()
        return carry

    lax.fori_loop(1, n_dev, a2a_start, 0)
    for copy in second:
        copy.wait()
    far = tab_at(1 - x, 1 - y, c)
    across.append(send(far, far, c_peer))
    for group in tab_plane:
        group[2].wait()
    lax.fori_loop(1, n_dev, a2a_wait, 0)
    for copy in across:
        copy.wait()


def expand_kernel(per_step, half_ref, tab_ref, out_ref, left_t, right):
    step = pl.program_id(0)
    width = left_t.shape[0]
    quarter = width // 4

    @pl.when(step == 0)
    def _():
        for q in range(4):
            left_t[q * quarter : (q + 1) * quarter, :] = tab_ref[q, 0].T
            right[:, q * quarter : (q + 1) * quarter] = tab_ref[q, 1]

    for k in range(per_step):
        weighted = left_t[...] * half_ref[step * per_step + k]
        out_ref[0, k] = jnp.dot(
            weighted, right[...], preferred_element_type=F32
        ).astype(BF)


def fast_body(integrals, screen, occupied, virtual, pair_index):
    n_pair, n_orb = lax.axis_size("pair"), lax.axis_size("orb")
    n_dev = n_pair * n_orb
    nz = n_pair // 2
    rows, width = virtual.shape
    pairs = pair_index.shape[1]
    i_count = occupied.shape[1]
    slots = integrals.shape[1]
    own_pairs = integrals.shape[0] // n_orb
    per_dev = rows // BLK
    share = pairs // nz
    j_own = i_count // n_pair
    lanes = own_pairs * i_count // n_orb
    sends = 3 + 3 * (nz - 1) + 8 + 1 + 4 * nz + 3
    vmem = pl.BlockSpec(memory_space=pltpu.VMEM)
    table, half = pl.pallas_call(
        functools.partial(exchange_kernel, (n_pair, n_orb, nz, own_pairs, slots)),
        out_shape=(
            jax.ShapeDtypeStruct((4, 2, pairs, width // 4), BF),
            jax.ShapeDtypeStruct((n_dev, j_own, lanes), F32),
        ),
        in_specs=[
            pl.BlockSpec(memory_space=pltpu.SMEM),
            pl.BlockSpec(memory_space=pltpu.HBM),
            pl.BlockSpec(memory_space=pltpu.HBM),
            pl.BlockSpec(memory_space=pltpu.HBM),
            vmem,
        ],
        out_specs=(vmem, vmem),
        scratch_shapes=[
            pltpu.VMEM((own_pairs * slots, BLK, BLK), BF),
            pltpu.VMEM((n_dev * per_dev, i_count, BLK), BF),
            pltpu.VMEM((4, rows, width // 4), BF),
            pltpu.VMEM((pairs, width // 4), BF),
            pltpu.VMEM((2, pairs, width // 4), BF),
            pltpu.VMEM((nz - 1, share, width // 4), BF),
            pltpu.VMEM((own_pairs, i_count, i_count), F32),
            pltpu.VMEM((n_dev, j_own, lanes), F32),
            pltpu.SemaphoreType.DMA,
            pltpu.SemaphoreType.DMA((1 + per_dev,)),
            pltpu.SemaphoreType.DMA((sends,)),
            pltpu.SemaphoreType.DMA((sends,)),
            pltpu.SemaphoreType.DMA((n_dev,)),
            pltpu.SemaphoreType.DMA((n_dev,)),
        ],
        compiler_params=pltpu.CompilerParams(
            collective_id=0, has_side_effects=True, vmem_limit_bytes=60 * 2**20
        ),
    )(
        screen.transpose(0, 2, 1),
        integrals.reshape(-1, BLK, BLK),
        occupied.T,
        virtual,
        pair_index,
    )
    k_own = i_count // n_orb
    half = half.reshape(n_dev, j_own, k_own, own_pairs).transpose(1, 2, 0, 3)
    half = half.reshape(j_own * k_own, 1, pairs).astype(BF)
    count = j_own * k_own
    per_step = 8
    return pl.pallas_call(
        functools.partial(expand_kernel, per_step),
        grid=(count // per_step,),
        out_shape=jax.ShapeDtypeStruct((1, count, width, width), BF),
        in_specs=[vmem, vmem],
        out_specs=pl.BlockSpec((1, per_step, width, width), lambda s: (0, s, 0, 0)),
        scratch_shapes=[pltpu.VMEM((width, pairs), BF), pltpu.VMEM((pairs, width), BF)],
        compiler_params=pltpu.CompilerParams(vmem_limit_bytes=32 * 2**20),
    )(half, table)


def plain_body(integrals, screen, occupied, virtual, pair_index):
    occ_all = lax.all_gather(occupied, ("pair", "orb"), axis=0, tiled=True)
    vir_all = lax.all_gather(virtual, ("pair", "orb"), axis=0, tiled=True)
    first_count = occ_all.shape[1] // lax.axis_size("orb")
    own_cols = lax.dynamic_slice_in_dim(
        occ_all, lax.axis_index("orb") * first_count, first_count, 1
    )
    block_count = occ_all.shape[0] // BLK

    def blocks_of(cols, index):
        hot = jax.nn.one_hot(index.reshape(-1), block_count, dtype=BF)
        taken = jnp.dot(
            hot, cols.reshape(block_count, -1), preferred_element_type=F32
        ).astype(BF)
        return taken.reshape(index.shape + (BLK, cols.shape[1]))

    coef_m = blocks_of(own_cols, screen[0])
    coef_n = blocks_of(occ_all, screen[1])
    half_one = jnp.einsum(
        "pkmn,pkmi->pkni", integrals, coef_m, preferred_element_type=F32
    ).astype(BF)
    half = jnp.einsum(
        "pknj,pkni->pji", coef_n, half_one, preferred_element_type=F32
    ).astype(BF)
    local_rows = half.reshape(half.shape[0], -1)
    owned = lax.all_to_all(local_rows, "pair", split_axis=1, concat_axis=0, tiled=True)
    left = vir_all[pair_index[0]]
    right = vir_all[pair_index[1]]
    weighted = (left[:, None, :].astype(F32) * owned[:, :, None].astype(F32)).astype(BF)
    width = weighted.shape[2]
    flat = weighted.reshape(weighted.shape[0], -1)
    result = lax.dot_general(
        flat, right, (((0,), (0,)), ((), ())), preferred_element_type=F32
    )
    return result.astype(BF).reshape(1, -1, width, width)


def body(*args):
    n_pair, n_orb = lax.axis_size("pair"), lax.axis_size("orb")
    fits = (
        n_orb == 4
        and n_pair in (4, 8)
        and args[2].shape[0] % BLK == 0
        and args[4].shape[1] == n_pair * args[0].shape[0]
    )
    return fast_body(*args) if fits else plain_body(*args)


def solution(mesh):
    placed = (
        P("pair", None, None, None),
        P(None, "pair", None),
        P(("pair", "orb"), None),
        P(("pair", "orb"), None),
        P(),
    )
    return jax.shard_map(
        body, mesh=mesh, in_specs=placed, out_specs=P("orb", "pair", None, None), check_vma=False
    )
```
